32 devices in a mesh: wide: 16 (over z, x, core), tm: 2 (over y).
Axes of the slice: x: 2, y: 2, z: 4, core: 2. Of those that a mesh axis runs over, the one named last changes fastest.
Arguments:
- voltages: int32 [256, 131072], P('wide', 'tm'), may hold values from -128 to 127
- taps: int32 [16, 1024], replicated, may hold values from -32 to 32
Outputs:
- visibility: float32 [256, 2, 512, 256], P('tm', None, 'wide')
The draws below stay inside these ranges and needn't reach their ends.
All inputs are finite; a program needn't handle non-finite values.
Results may differ from the reference program's by a relative error of at most 0.0024.
Values may be sent and summed in bfloat16 or wider, within the bound.
A program may use at most 64 MiB of HBM per device.

```python
import jax
import jax.numpy as jnp
from jax import lax

A = 256
C = 512
P_SIZE = 16
L = 1024
NSPEC = 128
SAMPLES = 131072


def place_ends(array, key, least, top_value):
    index_at = [jax.random.randint(jax.random.fold_in(key, axis), (), 0, length) for axis, length in enumerate(array.shape)]
    widest = array.shape.index(max(array.shape))
    next_to = index_at[:widest] + [(index_at[widest] + 1) % array.shape[widest]] + index_at[widest + 1:]
    return array.at[tuple(index_at)].set(least).at[tuple(next_to)].set(top_value)


def setup_inputs(seed: int = 0) -> dict:
    key_of = jax.random.split(jax.random.key(seed), 3)
    voltages = place_ends(jax.random.randint(key_of[0], (A, SAMPLES), -128, 128), jax.random.fold_in(key_of[0], 1), -128, 127).astype(jnp.int32)
    taps = place_ends(jax.random.randint(key_of[1], (P_SIZE, L), -32, 33), jax.random.fold_in(key_of[1], 1), -32, 32).astype(jnp.int32)
    return {"voltages": voltages, "taps": taps}


FIR_SCALE = 2.0 ** -12


def channelize(volt_row, taps_float):
    frames = volt_row.astype(jnp.bfloat16).astype(jnp.float32).reshape(NSPEC, L)
    padded = jnp.concatenate([jnp.zeros((P_SIZE - 1, L), jnp.float32), frames], axis=0)
    filtered = jnp.zeros((NSPEC, L), jnp.float32)
    for lag in range(P_SIZE):
        filtered = filtered + taps_float[lag] * padded[P_SIZE - 1 - lag:P_SIZE - 1 - lag + NSPEC]
    filtered = filtered * FIR_SCALE
    spectrum = jnp.fft.rfft(filtered, axis=-1)[:, :C] * (L ** -0.5)
    real_part = jnp.real(spectrum).astype(jnp.bfloat16)
    imag_part = jnp.imag(spectrum).astype(jnp.bfloat16)
    return jnp.concatenate([real_part.T, imag_part.T], axis=1)


def channel_gram(full_rows):
    full_float = full_rows.astype(jnp.float32)
    rotated = jnp.concatenate([full_float[:, NSPEC:], -full_float[:, :NSPEC]], axis=1)
    real_part = jnp.dot(full_float, full_float.T, preferred_element_type=jnp.float32)
    imag_part = jnp.dot(rotated, full_float.T, preferred_element_type=jnp.float32)
    return jnp.stack([real_part, imag_part], axis=0)


def reference(voltages, taps):
    taps_float = taps.astype(jnp.float32)
    spectra = lax.map(lambda volt_row: channelize(volt_row, taps_float), voltages)
    per_channel = lax.map(channel_gram, jnp.transpose(spectra, (1, 0, 2)))
    return jnp.transpose(per_channel, (2, 1, 0, 3)) * (1.0 / NSPEC)
```

```python
import functools

import jax
import jax.numpy as jnp
import ml_dtypes
import numpy as np
from jax import lax
from jax.experimental import pallas as pl
from jax.experimental.pallas import tpu as pltpu
from jax.sharding import PartitionSpec as P

FIR_SCALE = 2.0 ** (-12)
MESH = pl.DeviceIdType.MESH
SUBLANES = 8
LANES = 128
VMEM_BYTES = 56 * 1024 * 1024


def dft_tables(length, widen):
    half = length // 2
    group = half // 2 // widen
    sample = np.arange(half)
    tables = []
    for parity in range(2):
        channel = 2 * np.arange(half // 2).reshape(widen, group) + parity
        angle = 2.0 * np.pi / length * (channel[:, :, None] * sample % length)
        table = np.stack([np.cos(angle), -np.sin(angle)], axis=1)
        table = table.reshape(widen * 2 * group, half) * (FIR_SCALE * length ** (-0.5))
        high = table.astype(ml_dtypes.bfloat16)
        low = (table - high.astype(np.float64)).astype(ml_dtypes.bfloat16)
        tables.append(np.concatenate([high, high, low], axis=1))
    return np.stack(tables)


def spectra_kernel(widen, volt_ref, halo_ref, taps_ref, table_ref, out_ref, folded, product, turned):
    inputs = volt_ref.shape[0]
    lags, length = taps_ref.shape
    frames = volt_ref.shape[1] // length
    half = length // 2
    chunks = half // LANES
    groups = inputs // SUBLANES
    group = half // 2 // widen
    columns = 256
    step = 8

    def frame(s, rows, lane):
        if s >= 0:
            return volt_ref[rows, pl.ds(s * length + lane, LANES)].astype(jnp.float32)
        at = (s + lags - 1) * length + lane
        return halo_ref[rows, pl.ds(at, LANES)].astype(jnp.float32)

    @pl.loop(0, groups * chunks)
    def fir(index):
        g = index // chunks
        c = index % chunks
        rows = pl.ds(pl.multiple_of(g * SUBLANES, SUBLANES), SUBLANES)
        for first in range(0, frames, step):
            sums = []
            for part in range(2):
                lane = pl.multiple_of(c * LANES, LANES) + part * half
                window = {s: frame(s, rows, lane) for s in range(first - lags + 1, first + step)}
                taps = [
                    taps_ref[pl.ds(p, 1), pl.ds(lane, LANES)].astype(jnp.float32)
                    for p in range(lags)
                ]
                totals = []
                for s in range(first, first + step):
                    total = taps[0] * window[s]
                    for p in range(1, lags):
                        total = total + taps[p] * window[s - p]
                    totals.append(total)
                sums.append(totals)
            for i in range(step):
                at = pl.ds(g * (SUBLANES * frames) + first + i, SUBLANES, stride=frames)
                folded[c, at, :] = sums[0][i] + sums[1][i]
                folded[chunks + c, at, :] = sums[0][i] - sums[1][i]

    pairs = columns // LANES
    blocks = inputs * frames // columns
    low_lanes = lax.broadcasted_iota(jnp.int32, (group, LANES), 1) < frames
    for parity in range(2):

        @pl.loop(0, blocks)
        def dft(block):
            rows = pl.ds(pl.multiple_of(block * columns, columns), columns)
            high, low = [], []
            for c in range(chunks):
                value = folded[parity * chunks + c, rows, :]
                top = value.astype(jnp.bfloat16)
                high.append(top)
                low.append((value - top.astype(jnp.float32)).astype(jnp.bfloat16))
            operand = jnp.concatenate(high + low + high, axis=1)
            product[...] = lax.dot_general(
                table_ref[parity], operand, (((1,), (1,)), ((), ())),
                preferred_element_type=jnp.float32,
            )

            @pl.loop(0, widen)
            def turn(d):
                at = pl.multiple_of(d * 2 * group, SUBLANES)
                for pair in range(pairs):
                    lanes = pl.ds(pair * LANES, LANES)
                    re = product[pl.ds(at, group), lanes]
                    im = product[pl.ds(at + group, group), lanes]
                    first = jnp.where(low_lanes, re, pltpu.roll(im, frames, 1))
                    second = jnp.where(low_lanes, pltpu.roll(re, frames, 1), im)
                    a = (block * pairs + pair) * 2
                    base = d * (group * inputs) + a
                    turned[pl.ds(base, group, stride=inputs), :] = first
                    turned[pl.ds(base + 1, group, stride=inputs), :] = second

        @pl.loop(0, widen)
        def cast(d):
            rows = pl.ds(pl.multiple_of(d * (group * inputs), group * inputs), group * inputs)
            out_ref[d, pl.ds(parity * group * inputs, group * inputs), :] = turned[rows, :].astype(
                jnp.bfloat16
            )


def spectra_of(voltages, halo, taps, widen):
    inputs = voltages.shape[0]
    length = taps.shape[1]
    frames = voltages.shape[1] // length
    half = length // 2
    table = jnp.asarray(dft_tables(length, widen))
    rows = half // widen * inputs
    return pl.pallas_call(
        functools.partial(spectra_kernel, widen),
        out_shape=jax.ShapeDtypeStruct((widen, rows, 2 * frames), jnp.bfloat16),
        in_specs=[pl.BlockSpec(memory_space=pltpu.VMEM)] * 4,
        out_specs=pl.BlockSpec(memory_space=pltpu.VMEM),
        scratch_shapes=[
            pltpu.VMEM((2 * half // LANES, inputs * frames, LANES), jnp.float32),
            pltpu.VMEM((half, 256), jnp.float32),
            pltpu.VMEM((half // 2 * inputs, LANES), jnp.float32),
        ],
        compiler_params=pltpu.CompilerParams(vmem_limit_bytes=VMEM_BYTES),
        cost_estimate=pl.CostEstimate(
            flops=6 * half * length * inputs * frames, bytes_accessed=12 << 20, transcendentals=0
        ),
        name="spectra",
    )(voltages, halo, taps, table)


def flipped(index, bits):
    bit = 1
    while bit <= bits:
        if bits & bit:
            index = index + bit - 2 * bit * ((index // bit) % 2)
        bit *= 2
    return index


def send_order(widen):
    far = [i for i in range(widen // 2, widen)]
    near = [i for i in range(2, widen // 2)]
    order = [1]
    while far or near:
        order += far[:2] + near[:1]
        far, near = far[2:], near[1:]
    return order


def exchange_kernel(widen, ranks, spec_ref, out_ref, own_sem, send_wide, recv_wide, send_tm, recv_tm):
    w = lax.axis_index("wide")
    t = lax.axis_index("tm")
    order = send_order(widen)

    barrier = pltpu.get_barrier_semaphore()
    for i in order:
        pl.semaphore_signal(barrier, inc=1, device_id=(flipped(w, i), t), device_id_type=MESH)
    for r in range(1, ranks):
        pl.semaphore_signal(
            barrier, inc=1, device_id=(w, lax.rem(t + r, ranks)), device_id_type=MESH
        )
    pl.semaphore_wait(barrier, len(order) + ranks - 1)

    def onward(src_ref, i, r):
        return pltpu.make_async_remote_copy(
            src_ref=src_ref,
            dst_ref=out_ref.at[t, flipped(w, i)],
            send_sem=send_tm.at[i, r - 1],
            recv_sem=recv_tm.at[i, r - 1],
            device_id=(w, lax.rem(t + r, ranks)),
            device_id_type=MESH,
        )

    own = pltpu.make_async_copy(spec_ref.at[w], out_ref.at[t, w], own_sem)
    own.start()
    copies = []
    for r in range(1, ranks):
        copy = onward(spec_ref.at[w], 0, r)
        copy.start()
        copies.append(copy)
    across = []
    for i in order:
        partner = flipped(w, i)
        copy = pltpu.make_async_remote_copy(
            src_ref=spec_ref.at[partner],
            dst_ref=out_ref.at[t, w],
            send_sem=send_wide.at[i],
            recv_sem=recv_wide.at[i],
            device_id=(partner, t),
            device_id_type=MESH,
        )
        copy.start()
        across.append(copy)
    for i, copy in zip(order, across):
        copy.wait_recv()
        for r in range(1, ranks):
            passed = onward(out_ref.at[t, flipped(w, i)], i, r)
            passed.start()
            copies.append(passed)
    own.wait()
    for copy in across:
        copy.wait_send()
    for copy in copies:
        copy.wait()


def exchanged(spectra, widen, ranks):
    return pl.pallas_call(
        functools.partial(exchange_kernel, widen, ranks),
        out_shape=jax.ShapeDtypeStruct((ranks,) + spectra.shape, spectra.dtype),
        in_specs=[pl.BlockSpec(memory_space=pl.ANY)],
        out_specs=pl.BlockSpec(memory_space=pl.ANY),
        scratch_shapes=[
            pltpu.SemaphoreType.DMA(()),
            pltpu.SemaphoreType.DMA((widen,)),
            pltpu.SemaphoreType.DMA((widen,)),
            pltpu.SemaphoreType.DMA((widen, ranks - 1)),
            pltpu.SemaphoreType.DMA((widen, ranks - 1)),
        ],
        compiler_params=pltpu.CompilerParams(collective_id=0, has_side_effects=True),
        name="exchange",
    )(spectra)


def shards(voltages, taps):
    local_inputs = voltages.shape[0]
    lags, length = taps.shape
    frames = voltages.shape[1] // length
    widen = lax.axis_size("wide")
    ranks = lax.axis_size("tm")
    channels = length // 2 // widen
    norm = 1.0 / (frames * ranks)

    tail = voltages[:, (frames - lags + 1) * length :].astype(jnp.bfloat16)
    halo = lax.ppermute(tail, "tm", [(i, i + 1) for i in range(ranks - 1)])
    spectra = spectra_of(voltages, halo, taps, widen)
    full = exchanged(spectra, widen, ranks)
    return gram_rows(full, local_inputs, channels, norm)


def gram_rows(full, inputs, channels, norm):
    ranks, widen, rows, width = full.shape
    total = widen * inputs
    own = total // ranks
    step = SUBLANES
    group = channels // 2
    first = (lax.axis_index("tm") * (own // inputs)).astype(jnp.int32).reshape(1)
    pairs = step // 2
    split = full.reshape(ranks, widen, 2, group * inputs, width)

    def kernel(first_ref, even_ref, odd_ref, out_ref):
        own_from = first_ref[0]
        lane = lax.broadcasted_iota(jnp.int32, (own, width), 1)
        sign = jnp.where(lane < width // 2, norm, -norm)
        for k in range(step):
            ref = (even_ref, odd_ref)[k % 2]
            at = pl.ds(k // 2 * inputs, inputs)
            whole = jnp.concatenate(
                [ref[t, :, 0, at, :].reshape(total, width) for t in range(ranks)], axis=1
            )
            mine = [
                ref[t, pl.ds(own_from, own // inputs), 0, at, :].reshape(own, width)
                for t in range(ranks)
            ]
            rotated = [
                (pltpu.roll(x.astype(jnp.float32), width // 2, 1) * sign).astype(jnp.bfloat16)
                for x in mine
            ]
            scaled = [(x.astype(jnp.float32) * norm).astype(jnp.bfloat16) for x in mine]
            left = jnp.concatenate(
                [jnp.concatenate(scaled, axis=1), jnp.concatenate(rotated, axis=1)], axis=0
            )
            gram = lax.dot_general(
                left, whole, (((1,), (1,)), ((), ())), preferred_element_type=jnp.float32
            )
            out_ref[:, 0, k, :] = gram[:own]
            out_ref[:, 1, k, :] = gram[own:]

    block = (ranks, widen, 1, pairs * inputs, width)
    return pl.pallas_call(
        kernel,
        grid=(channels // step,),
        out_shape=jax.ShapeDtypeStruct((own, 2, channels, total), jnp.float32),
        in_specs=[
            pl.BlockSpec(memory_space=pltpu.SMEM),
            pl.BlockSpec(block, lambda i: (0, 0, 0, i, 0)),
            pl.BlockSpec(block, lambda i: (0, 0, 1, i, 0)),
        ],
        out_specs=pl.BlockSpec((own, 2, step, total), lambda i: (0, 0, i, 0)),
        compiler_params=pltpu.CompilerParams(vmem_limit_bytes=VMEM_BYTES),
        name="gram",
    )(first, split, split)


def solution(mesh):
    placed = (P("wide", "tm"), P())
    return jax.shard_map(
        shards, mesh=mesh, in_specs=placed, out_specs=P("tm", None, "wide", None), check_vma=False
    )
```

```python
import functools

import jax
import jax.numpy as jnp
import ml_dtypes
import numpy as np
from jax import lax
from jax.experimental import pallas as pl
from jax.experimental.pallas import tpu as pltpu
from jax.sharding import PartitionSpec as P

FIR_SCALE = 2.0 ** (-12)
MESH = pl.DeviceIdType.MESH
SUBLANES = 8
LANES = 128
STEP = 16
COLUMNS = 256
WINDOW = 8
VMEM_BYTES = 56 * 1024 * 1024


def dft_tables(length, widen):
    half = length // 2
    group = half // 2 // widen
    sample = np.arange(half)
    tables = []
    for parity in range(2):
        channel = 2 * np.arange(half // 2).reshape(widen, group) + parity
        angle = 2.0 * np.pi / length * (channel[:, :, None] * sample % length)
        table = np.stack([np.cos(angle), -np.sin(angle)], axis=1)
        table = table.reshape(widen * 2 * group, half) * (FIR_SCALE * length ** (-0.5))
        high = table.astype(ml_dtypes.bfloat16)
        low = (table - high.astype(np.float64)).astype(ml_dtypes.bfloat16)
        tables.append(np.concatenate([high, high, low], axis=1))
    return np.stack(tables)


def flipped(index, bits):
    bit = 1
    while bit <= bits:
        if bits & bit:
            index = index + bit - 2 * bit * ((index // bit) % 2)
        bit *= 2
    return index


def send_order(widen):
    far = [i for i in range(widen // 2, widen)]
    near = [i for i in range(2, widen // 2)]
    order = [1]
    while far or near:
        order += far[:2] + near[:1]
        far, near = far[2:], near[1:]
    return order


def spectra_kernel(
    widen, ranks, volt_ref, taps_ref, table_hbm, out_ref,
    tail, halo, before, table_ref, folded, turned, spec,
    table_sem, own_sem, halo_sems, send_wide, recv_wide, send_tm, recv_tm,
):
    w = lax.axis_index("wide")
    t = lax.axis_index("tm")
    inputs = volt_ref.shape[0]
    lags, length = taps_ref.shape
    frames = volt_ref.shape[1] // length
    half = length // 2
    chunks = half // LANES
    groups = inputs // SUBLANES
    group = half // 2 // widen
    order = send_order(widen)

    barrier = pltpu.get_barrier_semaphore()
    for i in order:
        pl.semaphore_signal(barrier, inc=1, device_id=(flipped(w, i), t), device_id_type=MESH)
    for r in range(1, ranks):
        pl.semaphore_signal(
            barrier, inc=1, device_id=(w, lax.rem(t + r, ranks)), device_id_type=MESH
        )
    load_table = pltpu.make_async_copy(table_hbm, table_ref, table_sem)
    load_table.start()
    from_frame = (frames - lags + 1) * length
    for p in range(lags - 1):
        at = pl.ds(p * length, length)
        tail[:, at] = volt_ref[:, pl.ds(from_frame + p * length, length)].astype(jnp.bfloat16)
    pl.semaphore_wait(barrier, len(order) + ranks - 1)

    halo_copy = pltpu.make_async_remote_copy(
        src_ref=tail, dst_ref=halo, send_sem=halo_sems.at[0], recv_sem=halo_sems.at[1],
        device_id=(w, lax.rem(t + 1, ranks)), device_id_type=MESH,
    )

    @pl.when(t < ranks - 1)
    def send_halo():
        halo_copy.start()

    def fir(index, first, frame):
        g = index // chunks
        c = index % chunks
        rows = pl.ds(pl.multiple_of(g * SUBLANES, SUBLANES), SUBLANES)
        sums = []
        for part in range(2):
            lane = pl.multiple_of(c * LANES, LANES) + part * half
            window = jnp.stack([frame(i - (lags - 1), rows, lane) for i in range(STEP + lags - 1)])
            total = None
            for p in range(lags):
                tap = taps_ref[pl.ds(p, 1), pl.ds(lane, LANES)].astype(jnp.float32)
                term = tap * window[lags - 1 - p : lags - 1 - p + STEP]
                total = term if total is None else total + term
            sums.append(total)
        for number, value in enumerate((sums[0] + sums[1], sums[0] - sums[1])):
            for i in range(STEP):
                at = pl.ds(g * (SUBLANES * frames) + first + i, SUBLANES, stride=frames)
                folded[number * chunks + c, at, :] = value[i]

    later = frames // STEP - 1

    @pl.loop(0, groups * chunks * later)
    def fir_later(index):
        first = (1 + index % later) * STEP

        def frame(s, rows, lane):
            return volt_ref[rows, pl.ds((first + s) * length + lane, LANES)].astype(jnp.float32)

        fir(index // later, first, frame)

    @pl.when(t == 0)
    def no_halo():
        before[...] = jnp.zeros_like(before)

    @pl.when(t > 0)
    def wait_halo():
        halo_copy.wait_recv()
        for p in range(lags - 1):
            at = pl.ds(p * length, length)
            before[:, at] = halo[:, at].astype(jnp.float32)

    @pl.loop(0, groups * chunks)
    def fir_first(index):
        def frame(s, rows, lane):
            if s < 0:
                at = pl.ds((s + lags - 1) * length + lane, LANES)
                return before[rows, at]
            return volt_ref[rows, pl.ds(s * length + lane, LANES)].astype(jnp.float32)

        fir(index, 0, frame)

    load_table.wait()
    pairs = COLUMNS // LANES
    blocks = inputs * frames // COLUMNS
    low_lanes = lax.broadcasted_iota(jnp.int32, (widen * group, LANES), 1) < frames

    def dft(parity, block):
        rows = pl.ds(pl.multiple_of(block * COLUMNS, COLUMNS), COLUMNS)
        high, low = [], []
        for c in range(chunks):
            value = folded[parity * chunks + c, rows, :]
            top = value.astype(jnp.bfloat16)
            high.append(top)
            low.append((value - top.astype(jnp.float32)).astype(jnp.bfloat16))
        operand = jnp.concatenate(high + low + high, axis=1)
        product = lax.dot_general(
            table_ref[parity], operand, (((1,), (1,)), ((), ())),
            preferred_element_type=jnp.float32,
        )
        for pair in range(pairs):
            part = product[:, pair * LANES : (pair + 1) * LANES]
            part = part.reshape(widen, 2, group, LANES)
            re = part[:, 0].reshape(widen * group, LANES)
            im = part[:, 1].reshape(widen * group, LANES)
            a = (block * pairs + pair) * 2
            turned[pl.ds(a, widen * group, stride=inputs), :] = jnp.where(
                low_lanes, re, pltpu.roll(im, frames, 1)
            )
            turned[pl.ds(a + 1, widen * group, stride=inputs), :] = jnp.where(
                low_lanes, pltpu.roll(re, frames, 1), im
            )

    def cast(parity):
        @pl.loop(0, widen)
        def one(d):
            rows = pl.ds(pl.multiple_of(d * (group * inputs), group * inputs), group * inputs)
            spec[d, parity] = turned[rows, :].astype(jnp.bfloat16)

    onward_copies, own_copies = [], []

    def pass_on(src_ref, parity, i):
        for r in range(1, ranks):
            copy = pltpu.make_async_remote_copy(
                src_ref=src_ref,
                dst_ref=out_ref.at[t, flipped(w, i), parity],
                send_sem=send_tm.at[parity, i, r - 1],
                recv_sem=recv_tm.at[parity, i, r - 1],
                device_id=(w, lax.rem(t + r, ranks)),
                device_id_type=MESH,
            )
            copy.start()
            onward_copies.append(copy)

    def own(parity):
        copy = pltpu.make_async_copy(
            spec.at[w, parity], out_ref.at[t, w, parity], own_sem.at[parity]
        )
        copy.start()
        own_copies.append(copy)
        pass_on(spec.at[w, parity], parity, 0)

    def across(parity, i):
        return pltpu.make_async_remote_copy(
            src_ref=spec.at[flipped(w, i), parity],
            dst_ref=out_ref.at[t, w, parity],
            send_sem=send_wide.at[parity, i],
            recv_sem=recv_wide.at[parity, i],
            device_id=(flipped(w, i), t),
            device_id_type=MESH,
        )

    sequence = [(parity, i) for parity in range(2) for i in order]
    started = []

    def start_next(limit):
        if len(started) < limit:
            copy = across(*sequence[len(started)])
            copy.start()
            started.append(copy)

    def handle(number, limit):
        parity, i = sequence[number]
        started[number].wait_recv()
        pass_on(out_ref.at[t, flipped(w, i), parity], parity, i)
        start_next(limit)

    @pl.loop(0, blocks)
    def dft_even(block):
        dft(0, block)

    cast(0)
    for _ in range(WINDOW):
        start_next(len(order))
    own(0)
    handled = 0
    for block in range(blocks):
        dft(1, block)
        handle(handled, len(order))
        handled += 1
    cast(1)
    own(1)
    while len(started) < handled + WINDOW:
        start_next(len(sequence))
    while handled < len(sequence):
        handle(handled, len(sequence))
        handled += 1

    for copy in own_copies:
        copy.wait()
    for copy in started:
        copy.wait_send()
    for copy in onward_copies:
        copy.wait()

    @pl.when(t < ranks - 1)
    def halo_sent():
        halo_copy.wait_send()


def exchanged_spectra(voltages, taps, widen, ranks):
    inputs = voltages.shape[0]
    lags, length = taps.shape
    frames = voltages.shape[1] // length
    half = length // 2
    table = jnp.asarray(dft_tables(length, widen))
    block = (2, half // 2 // widen * inputs, 2 * frames)
    halo_shape = (inputs, (lags - 1) * length)
    return pl.pallas_call(
        functools.partial(spectra_kernel, widen, ranks),
        out_shape=jax.ShapeDtypeStruct((ranks, widen) + block, jnp.bfloat16),
        in_specs=[
            pl.BlockSpec(memory_space=pltpu.VMEM),
            pl.BlockSpec(memory_space=pltpu.VMEM),
            pl.BlockSpec(memory_space=pl.ANY),
        ],
        out_specs=pl.BlockSpec(memory_space=pl.ANY),
        scratch_shapes=[
            pltpu.VMEM(halo_shape, jnp.bfloat16),
            pltpu.VMEM(halo_shape, jnp.bfloat16),
            pltpu.VMEM(halo_shape, jnp.float32),
            pltpu.VMEM(table.shape, jnp.bfloat16),
            pltpu.VMEM((2 * half // LANES, inputs * frames, LANES), jnp.float32),
            pltpu.VMEM((half // 2 * inputs, LANES), jnp.float32),
            pltpu.VMEM((widen,) + block, jnp.bfloat16),
            pltpu.SemaphoreType.DMA(()),
            pltpu.SemaphoreType.DMA((2,)),
            pltpu.SemaphoreType.DMA((2,)),
            pltpu.SemaphoreType.DMA((2, widen)),
            pltpu.SemaphoreType.DMA((2, widen)),
            pltpu.SemaphoreType.DMA((2, widen, ranks - 1)),
            pltpu.SemaphoreType.DMA((2, widen, ranks - 1)),
        ],
        compiler_params=pltpu.CompilerParams(
            collective_id=0, has_side_effects=True, vmem_limit_bytes=VMEM_BYTES
        ),
        name="spectra_exchange",
    )(voltages, taps, table)


def shards(voltages, taps):
    local_inputs = voltages.shape[0]
    lags, length = taps.shape
    frames = voltages.shape[1] // length
    widen = lax.axis_size("wide")
    ranks = lax.axis_size("tm")
    channels = length // 2 // widen
    norm = 1.0 / (frames * ranks)

    full = exchanged_spectra(voltages, taps, widen, ranks)
    return gram_rows(full, local_inputs, channels, norm)


def gram_rows(full, inputs, channels, norm):
    ranks, widen, _, _, width = full.shape
    total = widen * inputs
    own = total // ranks
    step = SUBLANES
    first = (lax.axis_index("tm") * (own // inputs)).astype(jnp.int32).reshape(1)
    pairs = step // 2

    def kernel(first_ref, even_ref, odd_ref, out_ref):
        own_from = first_ref[0]
        lane = lax.broadcasted_iota(jnp.int32, (own, width), 1)
        sign = jnp.where(lane < width // 2, norm, -norm)
        for k in range(step):
            ref = (even_ref, odd_ref)[k % 2]
            at = pl.ds(k // 2 * inputs, inputs)
            whole = jnp.concatenate(
                [ref[t, :, 0, at, :].reshape(total, width) for t in range(ranks)], axis=1
            )
            mine = [
                ref[t, pl.ds(own_from, own // inputs), 0, at, :].reshape(own, width)
                for t in range(ranks)
            ]
            rotated = [
                (pltpu.roll(x.astype(jnp.float32), width // 2, 1) * sign).astype(jnp.bfloat16)
                for x in mine
            ]
            scaled = [(x.astype(jnp.float32) * norm).astype(jnp.bfloat16) for x in mine]
            left = jnp.concatenate(
                [jnp.concatenate(scaled, axis=1), jnp.concatenate(rotated, axis=1)], axis=0
            )
            gram = lax.dot_general(
                left, whole, (((1,), (1,)), ((), ())), preferred_element_type=jnp.float32
            )
            out_ref[:, 0, k, :] = gram[:own]
            out_ref[:, 1, k, :] = gram[own:]

    block = (ranks, widen, 1, pairs * inputs, width)
    return pl.pallas_call(
        kernel,
        grid=(channels // step,),
        out_shape=jax.ShapeDtypeStruct((own, 2, channels, total), jnp.float32),
        in_specs=[
            pl.BlockSpec(memory_space=pltpu.SMEM),
            pl.BlockSpec(block, lambda i: (0, 0, 0, i, 0)),
            pl.BlockSpec(block, lambda i: (0, 0, 1, i, 0)),
        ],
        out_specs=pl.BlockSpec((own, 2, step, total), lambda i: (0, 0, i, 0)),
        compiler_params=pltpu.CompilerParams(vmem_limit_bytes=VMEM_BYTES),
        name="gram",
    )(first, full, full)


def solution(mesh):
    placed = (P("wide", "tm"), P())
    return jax.shard_map(
        shards, mesh=mesh, in_specs=placed, out_specs=P("tm", None, "wide", None), check_vma=False
    )
```

```python
import functools

import jax
import jax.numpy as jnp
import ml_dtypes
import numpy as np
from jax import lax
from jax.experimental import pallas as pl
from jax.experimental.pallas import tpu as pltpu
from jax.sharding import PartitionSpec as P

FIR_SCALE = 2.0 ** (-12)
MESH = pl.DeviceIdType.MESH
SUBLANES = 8
LANES = 128
STEP = 16
COLUMNS = 256
WINDOW = 8
VMEM_BYTES = 56 * 1024 * 1024


def dft_tables(length, widen):
    half = length // 2
    group = half // 2 // widen
    sample = np.arange(half)
    tables = []
    for parity in range(2):
        channel = 2 * np.arange(half // 2).reshape(widen, group) + parity
        angle = 2.0 * np.pi / length * (channel[:, :, None] * sample % length)
        table = np.stack([np.cos(angle), -np.sin(angle)], axis=1)
        table = table.reshape(widen * 2 * group, half) * (FIR_SCALE * length ** (-0.5))
        high = table.astype(ml_dtypes.bfloat16)
        low = (table - high.astype(np.float64)).astype(ml_dtypes.bfloat16)
        tables.append(np.concatenate([high, high, low], axis=1))
    return np.stack(tables)


def flipped(index, bits):
    bit = 1
    while bit <= bits:
        if bits & bit:
            index = index + bit - 2 * bit * ((index // bit) % 2)
        bit *= 2
    return index


def send_order(widen):
    far = [i for i in range(widen // 2, widen)]
    near = [i for i in range(2, widen // 2)]
    order = [1]
    while far or near:
        order += far[:2] + near[:1]
        far, near = far[2:], near[1:]
    return order


def spectra_kernel(
    widen, ranks, volt_ref, taps_ref, table_hbm, out_ref,
    tail, halo, before, table_ref, folded, product, turned, spec,
    table_sem, own_sem, halo_sems, send_wide, recv_wide, send_tm, recv_tm,
):
    w = lax.axis_index("wide")
    t = lax.axis_index("tm")
    inputs = volt_ref.shape[0]
    lags, length = taps_ref.shape
    frames = volt_ref.shape[1] // length
    half = length // 2
    chunks = half // LANES
    groups = inputs // SUBLANES
    group = half // 2 // widen
    order = send_order(widen)

    barrier = pltpu.get_barrier_semaphore()
    for i in order:
        pl.semaphore_signal(barrier, inc=1, device_id=(flipped(w, i), t), device_id_type=MESH)
    for r in range(1, ranks):
        pl.semaphore_signal(
            barrier, inc=1, device_id=(w, lax.rem(t + r, ranks)), device_id_type=MESH
        )
    load_table = pltpu.make_async_copy(table_hbm, table_ref, table_sem)
    load_table.start()
    from_frame = (frames - lags + 1) * length
    for p in range(lags - 1):
        at = pl.ds(p * length, length)
        tail[:, at] = volt_ref[:, pl.ds(from_frame + p * length, length)].astype(jnp.bfloat16)
    pl.semaphore_wait(barrier, len(order) + ranks - 1)

    halo_copy = pltpu.make_async_remote_copy(
        src_ref=tail, dst_ref=halo, send_sem=halo_sems.at[0], recv_sem=halo_sems.at[1],
        device_id=(w, lax.rem(t + 1, ranks)), device_id_type=MESH,
    )

    @pl.when(t < ranks - 1)
    def send_halo():
        halo_copy.start()

    span = frames // 2

    def fir(index, first, frame):
        g = index // chunks
        c = index % chunks
        rows = pl.ds(pl.multiple_of(g * SUBLANES, SUBLANES), SUBLANES)
        sums = []
        for part in range(2):
            lane = pl.multiple_of(c * LANES, LANES) + part * half
            window = jnp.stack([frame(i - (lags - 1), rows, lane) for i in range(STEP + lags - 1)])
            total = None
            for p in range(lags):
                tap = taps_ref[pl.ds(p, 1), pl.ds(lane, LANES)].astype(jnp.float32)
                term = tap * window[lags - 1 - p : lags - 1 - p + STEP]
                total = term if total is None else total + term
            sums.append(total)
        for number, value in enumerate((sums[0] + sums[1], sums[0] - sums[1])):
            for i in range(STEP):
                at = pl.ds(g * (SUBLANES * span) + first % span + i, SUBLANES, stride=span)
                folded[number * chunks + c, at, :] = value[i]

    def fir_later(first):
        @pl.loop(0, groups * chunks)
        def run(index):
            def frame(s, rows, lane):
                at = pl.ds((first + s) * length + lane, LANES)
                return volt_ref[rows, at].astype(jnp.float32)

            fir(index, first, frame)

    def fir_first():
        @pl.when(t == 0)
        def no_halo():
            before[...] = jnp.zeros_like(before)

        @pl.when(t > 0)
        def wait_halo():
            halo_copy.wait_recv()
            for p in range(lags - 1):
                at = pl.ds(p * length, length)
                before[:, at] = halo[:, at].astype(jnp.float32)

        @pl.loop(0, groups * chunks)
        def run(index):
            def frame(s, rows, lane):
                if s < 0:
                    return before[rows, pl.ds((s + lags - 1) * length + lane, LANES)]
                return volt_ref[rows, pl.ds(s * length + lane, LANES)].astype(jnp.float32)

            fir(index, 0, frame)

    tiles = COLUMNS // LANES
    blocks = inputs * span // COLUMNS
    lane_at = lax.broadcasted_iota(jnp.int32, (widen * group, LANES), 1)
    lower = lane_at < 2 * span
    even = (lane_at // span) % 2 == 0

    def dft(block):
        rows = pl.ds(pl.multiple_of(block * COLUMNS, COLUMNS), COLUMNS)
        for parity in range(2):
            high, low = [], []
            for c in range(chunks):
                value = folded[parity * chunks + c, rows, :]
                top = value.astype(jnp.bfloat16)
                high.append(top)
                low.append((value - top.astype(jnp.float32)).astype(jnp.bfloat16))
            operand = jnp.concatenate(high + low + high, axis=1)
            product[parity] = lax.dot_general(
                table_ref[parity], operand, (((1,), (1,)), ((), ())),
                preferred_element_type=jnp.float32,
            )
        for tile in range(tiles):
            parts = []
            for parity in range(2):
                part = product[parity, :, tile * LANES : (tile + 1) * LANES]
                part = part.reshape(widen, 2, group, LANES)
                parts.append(part[:, 0].reshape(widen * group, LANES))
                parts.append(part[:, 1].reshape(widen * group, LANES))
            x0, x1, x2, x3 = parts
            y0 = jnp.where(lower, x0, pltpu.roll(x2, 2 * span, 1))
            y2 = jnp.where(lower, pltpu.roll(x0, 2 * span, 1), x2)
            y1 = jnp.where(lower, x1, pltpu.roll(x3, 2 * span, 1))
            y3 = jnp.where(lower, pltpu.roll(x1, 2 * span, 1), x3)
            swapped = [
                jnp.where(even, y0, pltpu.roll(y1, span, 1)),
                jnp.where(even, pltpu.roll(y0, 3 * span, 1), y1),
                jnp.where(even, y2, pltpu.roll(y3, span, 1)),
                jnp.where(even, pltpu.roll(y2, 3 * span, 1), y3),
            ]
            for i in range(4):
                a = (block * tiles + tile) * 4 + i
                turned[pl.ds(a, widen * group, stride=inputs), :] = swapped[i]

    def cast(part):
        @pl.loop(0, widen)
        def one(d):
            rows = pl.ds(pl.multiple_of(d * (group * inputs), group * inputs), group * inputs)
            spec[d, part] = turned[rows, :].astype(jnp.bfloat16)

    onward_copies, own_copies = [], []

    def pass_on(src_ref, parity, i):
        for r in range(1, ranks):
            copy = pltpu.make_async_remote_copy(
                src_ref=src_ref,
                dst_ref=out_ref.at[t, flipped(w, i), parity],
                send_sem=send_tm.at[parity, i, r - 1],
                recv_sem=recv_tm.at[parity, i, r - 1],
                device_id=(w, lax.rem(t + r, ranks)),
                device_id_type=MESH,
            )
            copy.start()
            onward_copies.append(copy)

    def own(parity):
        copy = pltpu.make_async_copy(
            spec.at[w, parity], out_ref.at[t, w, parity], own_sem.at[parity]
        )
        copy.start()
        own_copies.append(copy)
        pass_on(spec.at[w, parity], parity, 0)

    def across(parity, i):
        return pltpu.make_async_remote_copy(
            src_ref=spec.at[flipped(w, i), parity],
            dst_ref=out_ref.at[t, w, parity],
            send_sem=send_wide.at[parity, i],
            recv_sem=recv_wide.at[parity, i],
            device_id=(flipped(w, i), t),
            device_id_type=MESH,
        )

    sequence = [(parity, i) for parity in range(2) for i in order]
    started = []

    def start_next(limit):
        if len(started) < limit:
            copy = across(*sequence[len(started)])
            copy.start()
            started.append(copy)

    def handle(number, limit):
        parity, i = sequence[number]
        started[number].wait_recv()
        pass_on(out_ref.at[t, flipped(w, i), parity], parity, i)
        start_next(limit)

    handled = 0

    def handle_some(count, limit):
        nonlocal handled
        for _ in range(count):
            handle(handled, limit)
            handled += 1

    for first in range(span, frames, STEP):
        fir_later(first)
    load_table.wait()

    @pl.loop(0, blocks)
    def dft_late(block):
        dft(block)

    cast(0)
    for _ in range(WINDOW):
        start_next(len(order))
    own(0)
    for first in range(STEP, span, STEP):
        fir_later(first)
    handle_some(3, len(order))
    fir_first()
    handle_some(2, len(order))

    @pl.loop(0, blocks)
    def dft_early(block):
        dft(block)

    handle_some(2, len(order))
    cast(1)
    own(1)
    while len(started) < handled + WINDOW:
        start_next(len(sequence))
    handle_some(len(sequence) - handled, len(sequence))

    for copy in own_copies:
        copy.wait()
    for copy in started:
        copy.wait_send()
    for copy in onward_copies:
        copy.wait()

    @pl.when(t < ranks - 1)
    def halo_sent():
        halo_copy.wait_send()


def exchanged_spectra(voltages, taps, widen, ranks):
    inputs = voltages.shape[0]
    lags, length = taps.shape
    frames = voltages.shape[1] // length
    half = length // 2
    table = jnp.asarray(dft_tables(length, widen))
    block = (2, half // 2 // widen * inputs, 2 * frames)
    halo_shape = (inputs, (lags - 1) * length)
    return pl.pallas_call(
        functools.partial(spectra_kernel, widen, ranks),
        out_shape=jax.ShapeDtypeStruct((ranks, widen) + block, jnp.bfloat16),
        in_specs=[
            pl.BlockSpec(memory_space=pltpu.VMEM),
            pl.BlockSpec(memory_space=pltpu.VMEM),
            pl.BlockSpec(memory_space=pl.ANY),
        ],
        out_specs=pl.BlockSpec(memory_space=pl.ANY),
        scratch_shapes=[
            pltpu.VMEM(halo_shape, jnp.bfloat16),
            pltpu.VMEM(halo_shape, jnp.bfloat16),
            pltpu.VMEM(halo_shape, jnp.float32),
            pltpu.VMEM(table.shape, jnp.bfloat16),
            pltpu.VMEM((2 * half // LANES, inputs * frames // 2, LANES), jnp.float32),
            pltpu.VMEM((2, half, COLUMNS), jnp.float32),
            pltpu.VMEM((half // 2 * inputs, LANES), jnp.float32),
            pltpu.VMEM((widen,) + block, jnp.bfloat16),
            pltpu.SemaphoreType.DMA(()),
            pltpu.SemaphoreType.DMA((2,)),
            pltpu.SemaphoreType.DMA((2,)),
            pltpu.SemaphoreType.DMA((2, widen)),
            pltpu.SemaphoreType.DMA((2, widen)),
            pltpu.SemaphoreType.DMA((2, widen, ranks - 1)),
            pltpu.SemaphoreType.DMA((2, widen, ranks - 1)),
        ],
        compiler_params=pltpu.CompilerParams(
            collective_id=0, has_side_effects=True, vmem_limit_bytes=VMEM_BYTES
        ),
        name="spectra_exchange",
    )(voltages, taps, table)


def shards(voltages, taps):
    local_inputs = voltages.shape[0]
    lags, length = taps.shape
    frames = voltages.shape[1] // length
    widen = lax.axis_size("wide")
    ranks = lax.axis_size("tm")
    channels = length // 2 // widen
    norm = 1.0 / (frames * ranks)

    full = exchanged_spectra(voltages, taps, widen, ranks)
    return gram_rows(full, local_inputs, channels, norm)


def gram_rows(full, inputs, channels, norm):
    ranks, widen, parts, _, width = full.shape
    total = widen * inputs
    own = total // ranks
    step = SUBLANES
    pairs = step // 2
    span = width // 4
    first = (lax.axis_index("tm") * (own // inputs)).astype(jnp.int32).reshape(1)
    pieces = [(t, part) for t in range(ranks) for part in range(parts)]

    def kernel(first_ref, ref, out_ref, turned):
        own_from = first_ref[0]
        lane = lax.broadcasted_iota(jnp.int32, (own, width), 1)
        real = (lane // span) % 2 == 0
        masks = [jnp.where(lane // (2 * span) == parity, norm, 0.0) for parity in range(2)]
        for j in range(pairs):
            at = pl.ds(j * inputs, inputs)
            whole = jnp.concatenate(
                [ref[t, :, part, at, :].reshape(total, width) for t, part in pieces], axis=1
            )
            rows = [[] for _ in range(4)]
            for t, part in pieces:
                x = ref[t, pl.ds(own_from, own // inputs), part, at, :].reshape(own, width)
                x = x.astype(jnp.float32)
                turn = jnp.where(real, pltpu.roll(x, 3 * span, 1), -pltpu.roll(x, span, 1))
                for parity in range(2):
                    rows[2 * parity].append((x * masks[parity]).astype(jnp.bfloat16))
                    rows[2 * parity + 1].append((turn * masks[parity]).astype(jnp.bfloat16))
            left = jnp.concatenate([jnp.concatenate(row, axis=1) for row in rows], axis=0)
            gram = lax.dot_general(
                left, whole, (((1,), (1,)), ((), ())), preferred_element_type=jnp.float32
            )
            for parity in range(2):
                for r in range(2):
                    top = (2 * parity + r) * own
                    for l in range(total // LANES):
                        turned[l, pl.ds(r * step + 2 * j + parity, own, stride=2 * step), :] = (
                            gram[top : top + own, l * LANES : (l + 1) * LANES]
                        )
        for l in range(total // LANES):
            out_ref[:, :, :, l * LANES : (l + 1) * LANES] = turned[l].reshape(own, 2, step, LANES)

    return pl.pallas_call(
        kernel,
        grid=(channels // step,),
        out_shape=jax.ShapeDtypeStruct((own, 2, channels, total), jnp.float32),
        in_specs=[
            pl.BlockSpec(memory_space=pltpu.SMEM),
            pl.BlockSpec((ranks, widen, parts, pairs * inputs, width), lambda i: (0, 0, 0, i, 0)),
        ],
        out_specs=pl.BlockSpec((own, 2, step, total), lambda i: (0, 0, i, 0)),
        scratch_shapes=[pltpu.VMEM((total // LANES, own * 2 * step, LANES), jnp.float32)],
        compiler_params=pltpu.CompilerParams(vmem_limit_bytes=VMEM_BYTES),
        name="gram",
    )(first, full)


def solution(mesh):
    placed = (P("wide", "tm"), P())
    return jax.shard_map(
        shards, mesh=mesh, in_specs=placed, out_specs=P("tm", None, "wide", None), check_vma=False
    )
```

```python
import functools

import jax
import jax.numpy as jnp
import ml_dtypes
import numpy as np
from jax import lax
from jax.experimental import pallas as pl
from jax.experimental.pallas import tpu as pltpu
from jax.sharding import PartitionSpec as P

FIR_SCALE = 2.0 ** (-12)
MESH = pl.DeviceIdType.MESH
SUBLANES = 8
LANES = 128
STEP = 16
COLUMNS = 256
WINDOW = 12
CARRIER = jnp.bfloat16
VMEM_BYTES = 56 * 1024 * 1024


def dft_tables(length, widen):
    half = length // 2
    group = half // 2 // widen
    sample = np.arange(half)
    tables = []
    for parity in range(2):
        channel = 2 * np.arange(half // 2).reshape(widen, group) + parity
        angle = 2.0 * np.pi / length * (channel[:, :, None] * sample % length)
        table = np.stack([np.cos(angle), -np.sin(angle)], axis=1)
        table = table.reshape(widen * 2 * group, half) * (FIR_SCALE * length ** (-0.5))
        high = table.astype(ml_dtypes.bfloat16)
        low = (table - high.astype(np.float64)).astype(ml_dtypes.bfloat16)
        tables.append(np.concatenate([high, high, low], axis=1))
    return np.stack(tables)


def flipped(index, bits):
    bit = 1
    while bit <= bits:
        if bits & bit:
            index = index + bit - 2 * bit * ((index // bit) % 2)
        bit *= 2
    return index


def send_order(widen):
    far = [i for i in range(widen // 2, widen)]
    near = [i for i in range(1, widen // 2)]
    order = []
    for i, other in enumerate(far):
        order += near[i : i + 1] + [other]
    return order


def spectra_kernel(
    widen, ranks, volt_ref, taps_ref, table_hbm, out_ref,
    tail, halo, before, table_ref, folded, product, turned, spec,
    table_sem, own_sem, halo_sems, send_wide, recv_wide, send_tm, recv_tm,
):
    w = lax.axis_index("wide")
    t = lax.axis_index("tm")
    inputs = volt_ref.shape[0]
    lags, length = taps_ref.shape
    frames = volt_ref.shape[1] // length
    half = length // 2
    chunks = half // LANES
    groups = inputs // SUBLANES
    group = half // 2 // widen
    order = send_order(widen)

    barrier = pltpu.get_barrier_semaphore()
    for i in order:
        pl.semaphore_signal(barrier, inc=1, device_id=(flipped(w, i), t), device_id_type=MESH)
    for r in range(1, ranks):
        pl.semaphore_signal(
            barrier, inc=1, device_id=(w, lax.rem(t + r, ranks)), device_id_type=MESH
        )
    load_table = pltpu.make_async_copy(table_hbm, table_ref, table_sem)
    load_table.start()
    from_frame = (frames - lags + 1) * length
    for p in range(lags - 1):
        at = pl.ds(p * length, length)
        tail[:, at] = volt_ref[:, pl.ds(from_frame + p * length, length)].astype(jnp.bfloat16)
    pl.semaphore_wait(barrier, len(order) + ranks - 1)

    halo_copy = pltpu.make_async_remote_copy(
        src_ref=tail, dst_ref=halo, send_sem=halo_sems.at[0], recv_sem=halo_sems.at[1],
        device_id=(w, lax.rem(t + 1, ranks)), device_id_type=MESH,
    )

    @pl.when(t < ranks - 1)
    def send_halo():
        halo_copy.start()

    span = frames // 2

    def fir(index, first, frame):
        g = index // chunks
        c = index % chunks
        rows = pl.ds(pl.multiple_of(g * SUBLANES, SUBLANES), SUBLANES)
        sums = []
        for part in range(2):
            lane = pl.multiple_of(c * LANES, LANES) + part * half
            window = jnp.stack([frame(i - (lags - 1), rows, lane) for i in range(STEP + lags - 1)])
            total = None
            for p in range(lags):
                tap = taps_ref[pl.ds(p, 1), pl.ds(lane, LANES)].astype(jnp.float32)
                term = tap * window[lags - 1 - p : lags - 1 - p + STEP]
                total = term if total is None else total + term
            sums.append(total)
        for number, value in enumerate((sums[0] + sums[1], sums[0] - sums[1])):
            for i in range(STEP):
                at = pl.ds(g * (SUBLANES * span) + first % span + i, SUBLANES, stride=span)
                folded[number * chunks + c, at, :] = value[i]

    def fir_later(first):
        @pl.loop(0, groups * chunks)
        def run(index):
            def frame(s, rows, lane):
                at = pl.ds((first + s) * length + lane, LANES)
                return volt_ref[rows, at].astype(jnp.float32)

            fir(index, first, frame)

    def fir_first():
        @pl.when(t == 0)
        def no_halo():
            before[...] = jnp.zeros_like(before)

        @pl.when(t > 0)
        def wait_halo():
            halo_copy.wait_recv()
            for p in range(lags - 1):
                at = pl.ds(p * length, length)
                before[:, at] = halo[:, at].astype(jnp.float32)

        @pl.loop(0, groups * chunks)
        def run(index):
            def frame(s, rows, lane):
                if s < 0:
                    return before[rows, pl.ds((s + lags - 1) * length + lane, LANES)]
                return volt_ref[rows, pl.ds(s * length + lane, LANES)].astype(jnp.float32)

            fir(index, 0, frame)

    tiles = COLUMNS // LANES
    blocks = inputs * span // COLUMNS
    lane_at = lax.broadcasted_iota(jnp.int32, (widen * group, LANES), 1)
    lower = lane_at < 2 * span
    even = (lane_at // span) % 2 == 0

    def dft(block):
        rows = pl.ds(pl.multiple_of(block * COLUMNS, COLUMNS), COLUMNS)
        for parity in range(2):
            high, low = [], []
            for c in range(chunks):
                value = folded[parity * chunks + c, rows, :]
                top = value.astype(jnp.bfloat16)
                high.append(top)
                low.append((value - top.astype(jnp.float32)).astype(jnp.bfloat16))
            operand = jnp.concatenate(high + low + high, axis=1)
            product[parity] = lax.dot_general(
                table_ref[parity], operand, (((1,), (1,)), ((), ())),
                preferred_element_type=jnp.float32,
            )
        for tile in range(tiles):
            parts = []
            for parity in range(2):
                part = product[parity, :, tile * LANES : (tile + 1) * LANES]
                part = part.reshape(widen, 2, group, LANES)
                parts.append(part[:, 0].reshape(widen * group, LANES))
                parts.append(part[:, 1].reshape(widen * group, LANES))
            x0, x1, x2, x3 = parts
            y0 = jnp.where(lower, x0, pltpu.roll(x2, 2 * span, 1))
            y2 = jnp.where(lower, pltpu.roll(x0, 2 * span, 1), x2)
            y1 = jnp.where(lower, x1, pltpu.roll(x3, 2 * span, 1))
            y3 = jnp.where(lower, pltpu.roll(x1, 2 * span, 1), x3)
            swapped = [
                jnp.where(even, y0, pltpu.roll(y1, span, 1)),
                jnp.where(even, pltpu.roll(y0, 3 * span, 1), y1),
                jnp.where(even, y2, pltpu.roll(y3, span, 1)),
                jnp.where(even, pltpu.roll(y2, 3 * span, 1), y3),
            ]
            for i in range(4):
                a = (block * tiles + tile) * 4 + i
                turned[pl.ds(a, widen * group, stride=inputs), :] = swapped[i]

    def cast(part):
        @pl.loop(0, widen)
        def one(d):
            rows = pl.ds(pl.multiple_of(d * (group * inputs), group * inputs), group * inputs)
            spec[d, part] = turned[rows, :].astype(jnp.bfloat16)

    onward_copies, own_copies = [], []

    def pass_on(src_ref, parity, i):
        for r in range(1, ranks):
            copy = pltpu.make_async_remote_copy(
                src_ref=src_ref,
                dst_ref=out_ref.at[t, flipped(w, i), parity],
                send_sem=send_tm.at[parity, i, r - 1],
                recv_sem=recv_tm.at[parity, i, r - 1],
                device_id=(w, lax.rem(t + r, ranks)),
                device_id_type=MESH,
            )
            copy.start()
            onward_copies.append(copy)

    def own(parity):
        copy = pltpu.make_async_copy(
            spec.at[w, parity], out_ref.at[t, w, parity], own_sem.at[parity]
        )
        copy.start()
        own_copies.append(copy)
        pass_on(spec.at[w, parity], parity, 0)

    def across(parity, i):
        return pltpu.make_async_remote_copy(
            src_ref=spec.at[flipped(w, i), parity],
            dst_ref=out_ref.at[t, w, parity],
            send_sem=send_wide.at[parity, i],
            recv_sem=recv_wide.at[parity, i],
            device_id=(flipped(w, i), t),
            device_id_type=MESH,
        )

    sequence = [(parity, i) for parity in range(2) for i in order]
    started = []

    def start_next(limit):
        if len(started) < limit:
            copy = across(*sequence[len(started)])
            copy.start()
            started.append(copy)

    def handle(number, limit):
        parity, i = sequence[number]
        started[number].wait_recv()
        pass_on(out_ref.at[t, flipped(w, i), parity], parity, i)
        start_next(limit)

    handled = 0

    def handle_some(count, limit):
        nonlocal handled
        for _ in range(count):
            handle(handled, limit)
            handled += 1

    for first in range(span, frames, STEP):
        fir_later(first)
    load_table.wait()

    @pl.loop(0, blocks)
    def dft_late(block):
        dft(block)

    cast(0)
    for _ in range(WINDOW):
        start_next(len(order))
    own(0)
    for first in range(STEP, span, STEP):
        fir_later(first)
    handle_some(3, len(order))
    fir_first()
    handle_some(2, len(order))

    @pl.loop(0, blocks)
    def dft_early(block):
        dft(block)

    handle_some(2, len(order))
    cast(1)
    own(1)
    while len(started) < handled + WINDOW:
        start_next(len(sequence))
    handle_some(len(sequence) - handled, len(sequence))

    for copy in own_copies:
        copy.wait()
    for copy in started:
        copy.wait_send()
    for copy in onward_copies:
        copy.wait()

    @pl.when(t < ranks - 1)
    def halo_sent():
        halo_copy.wait_send()


def exchanged_spectra(voltages, taps, widen, ranks):
    inputs = voltages.shape[0]
    lags, length = taps.shape
    frames = voltages.shape[1] // length
    half = length // 2
    table = jnp.asarray(dft_tables(length, widen))
    block = (2, half // 2 // widen * inputs, 2 * frames)
    halo_shape = (inputs, (lags - 1) * length)
    return pl.pallas_call(
        functools.partial(spectra_kernel, widen, ranks),
        out_shape=jax.ShapeDtypeStruct((ranks, widen) + block, jnp.bfloat16),
        in_specs=[
            pl.BlockSpec(memory_space=pltpu.VMEM),
            pl.BlockSpec(memory_space=pltpu.VMEM),
            pl.BlockSpec(memory_space=pl.ANY),
        ],
        out_specs=pl.BlockSpec(memory_space=pl.ANY),
        scratch_shapes=[
            pltpu.VMEM(halo_shape, jnp.bfloat16),
            pltpu.VMEM(halo_shape, jnp.bfloat16),
            pltpu.VMEM(halo_shape, jnp.float32),
            pltpu.VMEM(table.shape, jnp.bfloat16),
            pltpu.VMEM((2 * half // LANES, inputs * frames // 2, LANES), jnp.float32),
            pltpu.VMEM((2, half, COLUMNS), jnp.float32),
            pltpu.VMEM((half // 2 * inputs, LANES), jnp.float32),
            pltpu.VMEM((widen,) + block, jnp.bfloat16),
            pltpu.SemaphoreType.DMA(()),
            pltpu.SemaphoreType.DMA((2,)),
            pltpu.SemaphoreType.DMA((2,)),
            pltpu.SemaphoreType.DMA((2, widen)),
            pltpu.SemaphoreType.DMA((2, widen)),
            pltpu.SemaphoreType.DMA((2, widen, ranks - 1)),
            pltpu.SemaphoreType.DMA((2, widen, ranks - 1)),
        ],
        compiler_params=pltpu.CompilerParams(
            collective_id=0, has_side_effects=True, vmem_limit_bytes=VMEM_BYTES
        ),
        name="spectra_exchange",
    )(voltages, taps, table)


def shards(voltages, taps):
    local_inputs = voltages.shape[0]
    lags, length = taps.shape
    frames = voltages.shape[1] // length
    widen = lax.axis_size("wide")
    ranks = lax.axis_size("tm")
    channels = length // 2 // widen
    norm = 1.0 / (frames * ranks)

    full = exchanged_spectra(voltages, taps, widen, ranks)
    return gram_rows(full, local_inputs, channels, norm)


def gram_rows(full, inputs, channels, norm):
    ranks, widen, parts, _, width = full.shape
    total = widen * inputs
    own = total // ranks
    step = SUBLANES
    pairs = step // 2
    span = width // 4
    first = (lax.axis_index("tm") * (own // inputs)).astype(jnp.int32).reshape(1)

    tiles = total // LANES
    sides = own // inputs

    def kernel(first_ref, ref, out_ref):
        own_from = first_ref[0]
        flat = out_ref.reshape(own * 2 * tiles * step, LANES)

        def picked(parity, first, second, lower):
            if parity:
                first = pltpu.roll(first, 2 * span, 1)
            else:
                second = pltpu.roll(second, 2 * span, 1)
            return jnp.where(lower, first, second)

        def lanes(rows):
            return lax.broadcasted_iota(jnp.int32, (rows, width), 1)

        for j in range(pairs):
            at = pl.ds(j * inputs, inputs)
            for parity in range(2):
                whole, mine, turned = [], [], []
                for t in range(ranks):
                    halves = [
                        ref[t, :, h, at, :].reshape(total, width).astype(CARRIER) for h in range(2)
                    ]
                    whole.append(picked(parity, *halves, lanes(total) < 2 * span))
                    halves = [
                        ref[t, pl.ds(own_from, sides), h, at, :].reshape(own, width)
                        .astype(jnp.float32)
                        for h in range(2)
                    ]
                    x = picked(parity, *halves, lanes(own) < 2 * span)
                    real = (lanes(own) // span) % 2 == 0
                    mine.append(x)
                    turned.append(
                        jnp.where(real, pltpu.roll(x, 3 * span, 1), -pltpu.roll(x, span, 1))
                    )
                left = jnp.concatenate(
                    [jnp.concatenate(mine, axis=1), jnp.concatenate(turned, axis=1)], axis=0
                ).astype(jnp.bfloat16)
                right = jnp.concatenate(whole, axis=1).astype(jnp.bfloat16)
                gram = norm * lax.dot_general(
                    left, right, (((1,), (1,)), ((), ())), preferred_element_type=jnp.float32
                )
                for r in range(2):
                    for l in range(tiles):
                        base = (r * tiles + l) * step + 2 * j + parity
                        flat[pl.ds(base, own, stride=2 * tiles * step), :] = gram[
                            r * own : (r + 1) * own, l * LANES : (l + 1) * LANES
                        ]

    tiled = pl.pallas_call(
        kernel,
        grid=(channels // step,),
        out_shape=jax.ShapeDtypeStruct((own, 2, channels // step, tiles, step, LANES), jnp.float32),
        in_specs=[
            pl.BlockSpec(memory_space=pltpu.SMEM),
            pl.BlockSpec((ranks, widen, parts, pairs * inputs, width), lambda i: (0, 0, 0, i, 0)),
        ],
        out_specs=pl.BlockSpec((own, 2, 1, tiles, step, LANES), lambda i: (0, 0, i, 0, 0, 0)),
        compiler_params=pltpu.CompilerParams(vmem_limit_bytes=VMEM_BYTES),
        name="gram",
    )(first, full)
    return jnp.swapaxes(tiled, 3, 4).reshape(own, 2, channels, total)


def solution(mesh):
    placed = (P("wide", "tm"), P())
    return jax.shard_map(
        shards, mesh=mesh, in_specs=placed, out_specs=P("tm", None, "wide", None), check_vma=False
    )
```

```python
import functools

import jax
import jax.numpy as jnp
import ml_dtypes
import numpy as np
from jax import lax
from jax.experimental import pallas as pl
from jax.experimental.pallas import tpu as pltpu
from jax.sharding import PartitionSpec as P

FIR_SCALE = 2.0 ** (-12)
MESH = pl.DeviceIdType.MESH
SUBLANES = 8
LANES = 128
STEP = 16
COLUMNS = 256
WINDOW = 16
VMEM_BYTES = 56 * 1024 * 1024


def dft_tables(length, widen):
    half = length // 2
    group = half // 2 // widen
    sample = np.arange(half)
    tables = []
    for parity in range(2):
        channel = 2 * np.arange(half // 2).reshape(widen, group) + parity
        angle = 2.0 * np.pi / length * (channel[:, :, None] * sample % length)
        table = np.stack([np.cos(angle), -np.sin(angle)], axis=1)
        table = table.reshape(widen * 2 * group, half) * (FIR_SCALE * length ** (-0.5))
        high = table.astype(ml_dtypes.bfloat16)
        low = (table - high.astype(np.float64)).astype(ml_dtypes.bfloat16)
        tables.append(np.concatenate([high, high, low], axis=1))
    return np.stack(tables)


def flipped(index, bits):
    bit = 1
    while bit <= bits:
        if bits & bit:
            index = index + bit - 2 * bit * ((index // bit) % 2)
        bit *= 2
    return index


def send_order(widen):
    far = [i for i in range(widen // 2, widen)]
    near = [i for i in range(1, widen // 2)]
    order = []
    for i, other in enumerate(far):
        order += near[i : i + 1] + [other]
    return order


def spectra_kernel(
    widen, ranks, volt_hbm, taps_ref, table_hbm, out_ref,
    volt_ref, tail, halo, before, table_ref, folded, product, turned, spec,
    volt_sems, table_sem, own_sem, halo_sems, send_wide, recv_wide, send_tm, recv_tm,
):
    w = lax.axis_index("wide")
    t = lax.axis_index("tm")
    inputs = volt_ref.shape[0]
    lags, length = taps_ref.shape
    frames = volt_ref.shape[1] // length
    half = length // 2
    chunks = half // LANES
    groups = inputs // SUBLANES
    group = half // 2 // widen
    order = send_order(widen)

    barrier = pltpu.get_barrier_semaphore()
    for i in order:
        pl.semaphore_signal(barrier, inc=1, device_id=(flipped(w, i), t), device_id_type=MESH)
    for r in range(1, ranks):
        pl.semaphore_signal(
            barrier, inc=1, device_id=(w, lax.rem(t + r, ranks)), device_id_type=MESH
        )
    border = (frames // 2 - lags) * length
    loads = []
    for i, (start, size) in enumerate([(border, frames * length - border), (0, border)]):
        at = pl.ds(start, size)
        load = pltpu.make_async_copy(volt_hbm.at[:, at], volt_ref.at[:, at], volt_sems.at[i])
        load.start()
        loads.append(load)
    load_table = pltpu.make_async_copy(table_hbm, table_ref, table_sem)
    load_table.start()

    halo_copy = pltpu.make_async_remote_copy(
        src_ref=tail, dst_ref=halo, send_sem=halo_sems.at[0], recv_sem=halo_sems.at[1],
        device_id=(w, lax.rem(t + 1, ranks)), device_id_type=MESH,
    )

    span = frames // 2

    def fir(index, first, frame):
        g = index // chunks
        c = index % chunks
        rows = pl.ds(pl.multiple_of(g * SUBLANES, SUBLANES), SUBLANES)
        sums = []
        for part in range(2):
            lane = pl.multiple_of(c * LANES, LANES) + part * half
            window = jnp.stack([frame(i - (lags - 1), rows, lane) for i in range(STEP + lags - 1)])
            total = None
            for p in range(lags):
                tap = taps_ref[pl.ds(p, 1), pl.ds(lane, LANES)].astype(jnp.float32)
                term = tap * window[lags - 1 - p : lags - 1 - p + STEP]
                total = term if total is None else total + term
            sums.append(total)
        for number, value in enumerate((sums[0] + sums[1], sums[0] - sums[1])):
            for i in range(STEP):
                at = pl.ds(g * (SUBLANES * span) + first % span + i, SUBLANES, stride=span)
                folded[number * chunks + c, at, :] = value[i]

    def fir_later(first):
        @pl.loop(0, groups * chunks)
        def run(index):
            def frame(s, rows, lane):
                at = pl.ds((first + s) * length + lane, LANES)
                return volt_ref[rows, at].astype(jnp.float32)

            fir(index, first, frame)

    def fir_first():
        @pl.when(t == 0)
        def no_halo():
            before[...] = jnp.zeros_like(before)

        @pl.when(t > 0)
        def wait_halo():
            halo_copy.wait_recv()
            for p in range(lags - 1):
                at = pl.ds(p * length, length)
                before[:, at] = halo[:, at].astype(jnp.float32)

        @pl.loop(0, groups * chunks)
        def run(index):
            def frame(s, rows, lane):
                if s < 0:
                    return before[rows, pl.ds((s + lags - 1) * length + lane, LANES)]
                return volt_ref[rows, pl.ds(s * length + lane, LANES)].astype(jnp.float32)

            fir(index, 0, frame)

    tiles = COLUMNS // LANES
    blocks = inputs * span // COLUMNS
    lane_at = lax.broadcasted_iota(jnp.int32, (widen * group, LANES), 1)
    lower = lane_at < 2 * span
    even = (lane_at // span) % 2 == 0

    def dft(block):
        rows = pl.ds(pl.multiple_of(block * COLUMNS, COLUMNS), COLUMNS)
        for parity in range(2):
            high, low = [], []
            for c in range(chunks):
                value = folded[parity * chunks + c, rows, :]
                top = value.astype(jnp.bfloat16)
                high.append(top)
                low.append((value - top.astype(jnp.float32)).astype(jnp.bfloat16))
            operand = jnp.concatenate(high + low + high, axis=1)
            product[parity] = lax.dot_general(
                table_ref[parity], operand, (((1,), (1,)), ((), ())),
                preferred_element_type=jnp.float32,
            )
        for tile in range(tiles):
            parts = []
            for parity in range(2):
                part = product[parity, :, tile * LANES : (tile + 1) * LANES]
                part = part.reshape(widen, 2, group, LANES)
                parts.append(part[:, 0].reshape(widen * group, LANES))
                parts.append(part[:, 1].reshape(widen * group, LANES))
            x0, x1, x2, x3 = parts
            y0 = jnp.where(lower, x0, pltpu.roll(x2, 2 * span, 1))
            y2 = jnp.where(lower, pltpu.roll(x0, 2 * span, 1), x2)
            y1 = jnp.where(lower, x1, pltpu.roll(x3, 2 * span, 1))
            y3 = jnp.where(lower, pltpu.roll(x1, 2 * span, 1), x3)
            swapped = [
                jnp.where(even, y0, pltpu.roll(y1, span, 1)),
                jnp.where(even, pltpu.roll(y0, 3 * span, 1), y1),
                jnp.where(even, y2, pltpu.roll(y3, span, 1)),
                jnp.where(even, pltpu.roll(y2, 3 * span, 1), y3),
            ]
            for i in range(4):
                a = (block * tiles + tile) * 4 + i
                turned[pl.ds(a, widen * group, stride=inputs), :] = swapped[i]

    def cast(part):
        @pl.loop(0, widen)
        def one(d):
            rows = pl.ds(pl.multiple_of(d * (group * inputs), group * inputs), group * inputs)
            spec[d, part] = turned[rows, :].astype(jnp.bfloat16)

    onward_copies, own_copies = [], []

    def pass_on(src_ref, parity, i):
        for r in range(1, ranks):
            copy = pltpu.make_async_remote_copy(
                src_ref=src_ref,
                dst_ref=out_ref.at[t, flipped(w, i), parity],
                send_sem=send_tm.at[parity, i, r - 1],
                recv_sem=recv_tm.at[parity, i, r - 1],
                device_id=(w, lax.rem(t + r, ranks)),
                device_id_type=MESH,
            )
            copy.start()
            onward_copies.append(copy)

    def own(parity):
        copy = pltpu.make_async_copy(
            spec.at[w, parity], out_ref.at[t, w, parity], own_sem.at[parity]
        )
        copy.start()
        own_copies.append(copy)
        pass_on(spec.at[w, parity], parity, 0)

    def across(parity, i):
        return pltpu.make_async_remote_copy(
            src_ref=spec.at[flipped(w, i), parity],
            dst_ref=out_ref.at[t, w, parity],
            send_sem=send_wide.at[parity, i],
            recv_sem=recv_wide.at[parity, i],
            device_id=(flipped(w, i), t),
            device_id_type=MESH,
        )

    sequence = [(parity, i) for parity in range(2) for i in order]
    started = []

    def start_next(limit):
        if len(started) < limit:
            copy = across(*sequence[len(started)])
            copy.start()
            started.append(copy)

    def handle(number, limit):
        parity, i = sequence[number]
        started[number].wait_recv()
        pass_on(out_ref.at[t, flipped(w, i), parity], parity, i)
        start_next(limit)

    handled = 0

    def handle_some(count, limit):
        nonlocal handled
        for _ in range(count):
            handle(handled, limit)
            handled += 1

    loads[0].wait()
    from_frame = (frames - lags + 1) * length
    for p in range(lags - 1):
        at = pl.ds(p * length, length)
        tail[:, at] = volt_ref[:, pl.ds(from_frame + p * length, length)].astype(jnp.bfloat16)
    fir_later(span)
    pl.semaphore_wait(barrier, len(order) + ranks - 1)

    @pl.when(t < ranks - 1)
    def send_halo():
        halo_copy.start()

    for first in range(span + STEP, frames, STEP):
        fir_later(first)
    load_table.wait()

    @pl.loop(0, blocks)
    def dft_late(block):
        dft(block)

    cast(0)
    for _ in range(WINDOW):
        start_next(len(order))
    own(0)
    loads[1].wait()
    for first in range(STEP, span, STEP):
        fir_later(first)
    handle_some(3, len(order))
    fir_first()
    handle_some(2, len(order))

    @pl.loop(0, blocks)
    def dft_early(block):
        dft(block)

    handle_some(2, len(order))
    cast(1)
    own(1)
    while len(started) < handled + WINDOW:
        start_next(len(sequence))
    handle_some(len(sequence) - handled, len(sequence))

    for copy in own_copies:
        copy.wait()
    for copy in started:
        copy.wait_send()
    for copy in onward_copies:
        copy.wait()

    @pl.when(t < ranks - 1)
    def halo_sent():
        halo_copy.wait_send()


def exchanged_spectra(voltages, taps, widen, ranks):
    inputs = voltages.shape[0]
    lags, length = taps.shape
    frames = voltages.shape[1] // length
    half = length // 2
    table = jnp.asarray(dft_tables(length, widen))
    block = (2, half // 2 // widen * inputs, 2 * frames)
    halo_shape = (inputs, (lags - 1) * length)
    return pl.pallas_call(
        functools.partial(spectra_kernel, widen, ranks),
        out_shape=jax.ShapeDtypeStruct((ranks, widen) + block, jnp.bfloat16),
        in_specs=[
            pl.BlockSpec(memory_space=pl.ANY),
            pl.BlockSpec(memory_space=pltpu.VMEM),
            pl.BlockSpec(memory_space=pl.ANY),
        ],
        out_specs=pl.BlockSpec(memory_space=pl.ANY),
        scratch_shapes=[
            pltpu.VMEM(voltages.shape, jnp.int32),
            pltpu.VMEM(halo_shape, jnp.bfloat16),
            pltpu.VMEM(halo_shape, jnp.bfloat16),
            pltpu.VMEM(halo_shape, jnp.float32),
            pltpu.VMEM(table.shape, jnp.bfloat16),
            pltpu.VMEM((2 * half // LANES, inputs * frames // 2, LANES), jnp.float32),
            pltpu.VMEM((2, half, COLUMNS), jnp.float32),
            pltpu.VMEM((half // 2 * inputs, LANES), jnp.float32),
            pltpu.VMEM((widen,) + block, jnp.bfloat16),
            pltpu.SemaphoreType.DMA((2,)),
            pltpu.SemaphoreType.DMA(()),
            pltpu.SemaphoreType.DMA((2,)),
            pltpu.SemaphoreType.DMA((2,)),
            pltpu.SemaphoreType.DMA((2, widen)),
            pltpu.SemaphoreType.DMA((2, widen)),
            pltpu.SemaphoreType.DMA((2, widen, ranks - 1)),
            pltpu.SemaphoreType.DMA((2, widen, ranks - 1)),
        ],
        compiler_params=pltpu.CompilerParams(
            collective_id=0, has_side_effects=True, vmem_limit_bytes=VMEM_BYTES
        ),
        name="spectra_exchange",
    )(voltages, taps, table)


def shards(voltages, taps):
    local_inputs = voltages.shape[0]
    lags, length = taps.shape
    frames = voltages.shape[1] // length
    widen = lax.axis_size("wide")
    ranks = lax.axis_size("tm")
    channels = length // 2 // widen
    norm = 1.0 / (frames * ranks)

    full = exchanged_spectra(voltages, taps, widen, ranks)
    return gram_rows(full, local_inputs, channels, norm)


def gram_rows(full, inputs, channels, norm):
    ranks, widen, parts, _, width = full.shape
    total = widen * inputs
    own = total // ranks
    step = SUBLANES
    pairs = step // 2
    span = width // 4
    first = (lax.axis_index("tm") * (own // inputs)).astype(jnp.int32).reshape(1)

    tiles = total // LANES
    sides = own // inputs
    pieces = [(t, h) for t in range(ranks) for h in range(parts)]

    def kernel(first_ref, ref, out_ref):
        own_from = first_ref[0]
        flat = out_ref.reshape(own * 2 * tiles * step, LANES)

        source = lax.broadcasted_iota(jnp.int32, (width, 2 * width), 0)
        target = lax.broadcasted_iota(jnp.int32, (width, 2 * width), 1)
        lane = target % width
        partner = jnp.where((lane // span) % 2 == 0, lane + span, lane - span)
        swap = jnp.where((lane // span) % 2 == 0, 1.0, -1.0)
        swap = jnp.where(
            (source == partner) & (lane // (2 * span) == target // width), swap, 0.0
        ).astype(jnp.bfloat16)
        lane = lax.broadcasted_iota(jnp.int32, (own, width), 1)
        masks = [
            jnp.where(lane // (2 * span) == parity, 1.0, 0.0).astype(jnp.bfloat16)
            for parity in range(2)
        ]

        for j in range(pairs):
            at = pl.ds(j * inputs, inputs)
            whole = jnp.concatenate(
                [ref[t, :, h, at, :].reshape(total, width) for t, h in pieces], axis=1
            )
            mine = [
                ref[t, pl.ds(own_from, sides), h, at, :].reshape(own, width) for t, h in pieces
            ]
            swapped = lax.dot_general(
                jnp.concatenate(mine, axis=0), swap, (((1,), (0,)), ((), ())),
                preferred_element_type=jnp.float32,
            ).astype(jnp.bfloat16)
            left = []
            for parity in range(2):
                left.append(jnp.concatenate([x * masks[parity] for x in mine], axis=1))
                columns = swapped[:, parity * width : (parity + 1) * width]
                left.append(
                    jnp.concatenate(
                        [columns[i * own : (i + 1) * own] for i in range(len(pieces))], axis=1
                    )
                )
            gram = norm * lax.dot_general(
                jnp.concatenate(left, axis=0), whole, (((1,), (1,)), ((), ())),
                preferred_element_type=jnp.float32,
            )
            for parity in range(2):
                for r in range(2):
                    top = (2 * parity + r) * own
                    for l in range(tiles):
                        base = (r * tiles + l) * step + 2 * j + parity
                        flat[pl.ds(base, own, stride=2 * tiles * step), :] = gram[
                            top : top + own, l * LANES : (l + 1) * LANES
                        ]

    tiled = pl.pallas_call(
        kernel,
        grid=(channels // step,),
        out_shape=jax.ShapeDtypeStruct((own, 2, channels // step, tiles, step, LANES), jnp.float32),
        in_specs=[
            pl.BlockSpec(memory_space=pltpu.SMEM),
            pl.BlockSpec((ranks, widen, parts, pairs * inputs, width), lambda i: (0, 0, 0, i, 0)),
        ],
        out_specs=pl.BlockSpec((own, 2, 1, tiles, step, LANES), lambda i: (0, 0, i, 0, 0, 0)),
        compiler_params=pltpu.CompilerParams(vmem_limit_bytes=VMEM_BYTES),
        name="gram",
    )(first, full)
    return jnp.swapaxes(tiled, 3, 4).reshape(own, 2, channels, total)


def solution(mesh):
    placed = (P("wide", "tm"), P())
    return jax.shard_map(
        shards, mesh=mesh, in_specs=placed, out_specs=P("tm", None, "wide", None), check_vma=False
    )
```

```python
import functools

import jax
import jax.numpy as jnp
import ml_dtypes
import numpy as np
from jax import lax
from jax.experimental import pallas as pl
from jax.experimental.pallas import tpu as pltpu
from jax.sharding import PartitionSpec as P

FIR_SCALE = 2.0 ** (-12)
MESH = pl.DeviceIdType.MESH
SUBLANES = 8
LANES = 128
STEP = 16
COLUMNS = 256
WINDOW = 16
VMEM_BYTES = 56 * 1024 * 1024


def dft_tables(length, widen):
    half = length // 2
    group = half // 2 // widen
    sample = np.arange(half)
    tables = []
    for parity in range(2):
        channel = 2 * np.arange(half // 2).reshape(widen, group) + parity
        angle = 2.0 * np.pi / length * (channel[:, :, None] * sample % length)
        table = np.stack([np.cos(angle), -np.sin(angle)], axis=1)
        table = table.reshape(widen * 2 * group, half) * (FIR_SCALE * length ** (-0.5))
        high = table.astype(ml_dtypes.bfloat16)
        low = (table - high.astype(np.float64)).astype(ml_dtypes.bfloat16)
        tables.append(np.concatenate([high, high, low], axis=1))
    return np.stack(tables)


def flipped(index, bits):
    bit = 1
    while bit <= bits:
        if bits & bit:
            index = index + bit - 2 * bit * ((index // bit) % 2)
        bit *= 2
    return index


def send_order(widen):
    far = [i for i in range(widen // 2, widen)]
    near = [i for i in range(1, widen // 2)]
    order = []
    for i, other in enumerate(far):
        order += near[i : i + 1] + [other]
    return order


def exchanged_sublanes(rows):
    axis = rows[0].ndim - 2
    sublane = lax.broadcasted_iota(jnp.int32, rows[0].shape, axis)
    for d in (4, 2, 1):
        low = (sublane // d) % 2 == 0
        new = list(rows)
        for i in range(SUBLANES):
            if i & d == 0:
                x, y = rows[i], rows[i + d]
                new[i] = jnp.where(low, x, pltpu.roll(y, d, axis))
                new[i + d] = jnp.where(low, pltpu.roll(x, SUBLANES - d, axis), y)
        rows = new
    return rows


def spectra_kernel(
    widen, ranks, volt_hbm, taps_ref, table_hbm, out_ref,
    volt_ref, tail, halo, before, table_ref, folded, product, turned, spec,
    volt_sems, table_sem, own_sem, halo_sems, send_wide, recv_wide, send_tm, recv_tm,
):
    w = lax.axis_index("wide")
    t = lax.axis_index("tm")
    inputs = volt_ref.shape[0]
    lags, length = taps_ref.shape
    frames = volt_ref.shape[1] // length
    half = length // 2
    chunks = half // LANES
    groups = inputs // SUBLANES
    group = half // 2 // widen
    order = send_order(widen)

    barrier = pltpu.get_barrier_semaphore()
    for i in order:
        pl.semaphore_signal(barrier, inc=1, device_id=(flipped(w, i), t), device_id_type=MESH)
    for r in range(1, ranks):
        pl.semaphore_signal(
            barrier, inc=1, device_id=(w, lax.rem(t + r, ranks)), device_id_type=MESH
        )
    border = (frames // 2 - lags) * length
    loads = []
    for i, (start, size) in enumerate([(border, frames * length - border), (0, border)]):
        at = pl.ds(start, size)
        load = pltpu.make_async_copy(volt_hbm.at[:, at], volt_ref.at[:, at], volt_sems.at[i])
        load.start()
        loads.append(load)
    load_table = pltpu.make_async_copy(table_hbm, table_ref, table_sem)
    load_table.start()

    halo_copy = pltpu.make_async_remote_copy(
        src_ref=tail, dst_ref=halo, send_sem=halo_sems.at[0], recv_sem=halo_sems.at[1],
        device_id=(w, lax.rem(t + 1, ranks)), device_id_type=MESH,
    )

    span = frames // 2

    def fir(index, first, frame):
        g = index // chunks
        c = index % chunks
        rows = pl.ds(pl.multiple_of(g * SUBLANES, SUBLANES), SUBLANES)
        sums = []
        for part in range(2):
            lane = pl.multiple_of(c * LANES, LANES) + part * half
            window = jnp.stack([frame(i - (lags - 1), rows, lane) for i in range(STEP + lags - 1)])
            total = None
            for p in range(lags):
                tap = taps_ref[pl.ds(p, 1), pl.ds(lane, LANES)].astype(jnp.float32)
                term = tap * window[lags - 1 - p : lags - 1 - p + STEP]
                total = term if total is None else total + term
            sums.append(total)
        for number, value in enumerate((sums[0] + sums[1], sums[0] - sums[1])):
            for b in range(0, STEP, SUBLANES):
                lines = exchanged_sublanes([value[b + i] for i in range(SUBLANES)])
                for i in range(SUBLANES):
                    at = pl.ds(first % span + b, SUBLANES)
                    folded[number * chunks + c, g * SUBLANES + i, at, :] = lines[i]

    def fir_later(first):
        @pl.loop(0, groups * chunks)
        def run(index):
            def frame(s, rows, lane):
                at = pl.ds((first + s) * length + lane, LANES)
                return volt_ref[rows, at].astype(jnp.float32)

            fir(index, first, frame)

    def fir_first():
        @pl.when(t == 0)
        def no_halo():
            before[...] = jnp.zeros_like(before)

        @pl.when(t > 0)
        def wait_halo():
            halo_copy.wait_recv()
            for p in range(lags - 1):
                at = pl.ds(p * length, length)
                before[:, at] = halo[:, at].astype(jnp.float32)

        @pl.loop(0, groups * chunks)
        def run(index):
            def frame(s, rows, lane):
                if s < 0:
                    return before[rows, pl.ds((s + lags - 1) * length + lane, LANES)]
                return volt_ref[rows, pl.ds(s * length + lane, LANES)].astype(jnp.float32)

            fir(index, 0, frame)

    tiles = COLUMNS // LANES
    blocks = inputs * span // COLUMNS
    lane_at = lax.broadcasted_iota(jnp.int32, (widen * group, LANES), 1)
    lower = lane_at < 2 * span
    even = (lane_at // span) % 2 == 0

    def dft(block):
        rows = pl.ds(block * SUBLANES, SUBLANES)
        for parity in range(2):
            high, low = [], []
            for c in range(chunks):
                value = folded[parity * chunks + c, rows].reshape(COLUMNS, LANES)
                top = value.astype(jnp.bfloat16)
                high.append(top)
                low.append((value - top.astype(jnp.float32)).astype(jnp.bfloat16))
            operand = jnp.concatenate(high + low + high, axis=1)
            product[parity] = lax.dot_general(
                table_ref[parity], operand, (((1,), (1,)), ((), ())),
                preferred_element_type=jnp.float32,
            )
        lines = []
        for tile in range(tiles):
            parts = []
            for parity in range(2):
                part = product[parity, :, tile * LANES : (tile + 1) * LANES]
                part = part.reshape(widen, 2, group, LANES)
                parts.append(part[:, 0].reshape(widen * group, LANES))
                parts.append(part[:, 1].reshape(widen * group, LANES))
            x0, x1, x2, x3 = parts
            y0 = jnp.where(lower, x0, pltpu.roll(x2, 2 * span, 1))
            y2 = jnp.where(lower, pltpu.roll(x0, 2 * span, 1), x2)
            y1 = jnp.where(lower, x1, pltpu.roll(x3, 2 * span, 1))
            y3 = jnp.where(lower, pltpu.roll(x1, 2 * span, 1), x3)
            lines += [
                jnp.where(even, y0, pltpu.roll(y1, span, 1)),
                jnp.where(even, pltpu.roll(y0, 3 * span, 1), y1),
                jnp.where(even, y2, pltpu.roll(y3, span, 1)),
                jnp.where(even, pltpu.roll(y2, 3 * span, 1), y3),
            ]
        lines = [x.reshape(widen * group // SUBLANES, SUBLANES, LANES) for x in lines]
        lines = exchanged_sublanes(lines)
        for j in range(SUBLANES):
            turned[:, j, block] = lines[j]

    def cast(part):
        @pl.loop(0, widen)
        def one(d):
            rows = pl.ds(d * (group // SUBLANES), group // SUBLANES)
            spec[d, part] = turned[rows].reshape(group * inputs, LANES).astype(jnp.bfloat16)

    onward_copies, own_copies = [], []

    def pass_on(src_ref, parity, i):
        for r in range(1, ranks):
            copy = pltpu.make_async_remote_copy(
                src_ref=src_ref,
                dst_ref=out_ref.at[t, flipped(w, i), parity],
                send_sem=send_tm.at[parity, i, r - 1],
                recv_sem=recv_tm.at[parity, i, r - 1],
                device_id=(w, lax.rem(t + r, ranks)),
                device_id_type=MESH,
            )
            copy.start()
            onward_copies.append(copy)

    def own(parity):
        copy = pltpu.make_async_copy(
            spec.at[w, parity], out_ref.at[t, w, parity], own_sem.at[parity]
        )
        copy.start()
        own_copies.append(copy)
        pass_on(spec.at[w, parity], parity, 0)

    def across(parity, i):
        return pltpu.make_async_remote_copy(
            src_ref=spec.at[flipped(w, i), parity],
            dst_ref=out_ref.at[t, w, parity],
            send_sem=send_wide.at[parity, i],
            recv_sem=recv_wide.at[parity, i],
            device_id=(flipped(w, i), t),
            device_id_type=MESH,
        )

    sequence = [(parity, i) for parity in range(2) for i in order]
    started = []

    def start_next(limit):
        if len(started) < limit:
            copy = across(*sequence[len(started)])
            copy.start()
            started.append(copy)

    def handle(number, limit):
        parity, i = sequence[number]
        started[number].wait_recv()
        pass_on(out_ref.at[t, flipped(w, i), parity], parity, i)
        start_next(limit)

    handled = 0

    def handle_some(count, limit):
        nonlocal handled
        for _ in range(count):
            handle(handled, limit)
            handled += 1

    loads[0].wait()
    from_frame = (frames - lags + 1) * length
    for p in range(lags - 1):
        at = pl.ds(p * length, length)
        tail[:, at] = volt_ref[:, pl.ds(from_frame + p * length, length)].astype(jnp.bfloat16)
    fir_later(span)
    pl.semaphore_wait(barrier, len(order) + ranks - 1)

    @pl.when(t < ranks - 1)
    def send_halo():
        halo_copy.start()

    for first in range(span + STEP, frames, STEP):
        fir_later(first)
    load_table.wait()

    @pl.loop(0, blocks)
    def dft_late(block):
        dft(block)

    cast(0)
    for _ in range(WINDOW):
        start_next(len(order))
    own(0)
    loads[1].wait()
    for first in range(STEP, span, STEP):
        fir_later(first)
    handle_some(3, len(order))
    fir_first()
    handle_some(2, len(order))

    @pl.loop(0, blocks)
    def dft_early(block):
        dft(block)

    handle_some(2, len(order))
    cast(1)
    own(1)
    while len(started) < handled + WINDOW:
        start_next(len(sequence))
    handle_some(len(sequence) - handled, len(sequence))

    for copy in own_copies:
        copy.wait()
    for copy in started:
        copy.wait_send()
    for copy in onward_copies:
        copy.wait()

    @pl.when(t < ranks - 1)
    def halo_sent():
        halo_copy.wait_send()


def exchanged_spectra(voltages, taps, widen, ranks):
    inputs = voltages.shape[0]
    lags, length = taps.shape
    frames = voltages.shape[1] // length
    half = length // 2
    table = jnp.asarray(dft_tables(length, widen))
    block = (2, half // 2 // widen * inputs, 2 * frames)
    halo_shape = (inputs, (lags - 1) * length)
    return pl.pallas_call(
        functools.partial(spectra_kernel, widen, ranks),
        out_shape=jax.ShapeDtypeStruct((ranks, widen) + block, jnp.bfloat16),
        in_specs=[
            pl.BlockSpec(memory_space=pl.ANY),
            pl.BlockSpec(memory_space=pltpu.VMEM),
            pl.BlockSpec(memory_space=pl.ANY),
        ],
        out_specs=pl.BlockSpec(memory_space=pl.ANY),
        scratch_shapes=[
            pltpu.VMEM(voltages.shape, jnp.int32),
            pltpu.VMEM(halo_shape, jnp.bfloat16),
            pltpu.VMEM(halo_shape, jnp.bfloat16),
            pltpu.VMEM(halo_shape, jnp.float32),
            pltpu.VMEM(table.shape, jnp.bfloat16),
            pltpu.VMEM((2 * half // LANES, inputs, frames // 2, LANES), jnp.float32),
            pltpu.VMEM((2, half, COLUMNS), jnp.float32),
            pltpu.VMEM(
                (half // 2 // SUBLANES, SUBLANES, inputs // SUBLANES, SUBLANES, LANES), jnp.float32
            ),
            pltpu.VMEM((widen,) + block, jnp.bfloat16),
            pltpu.SemaphoreType.DMA((2,)),
            pltpu.SemaphoreType.DMA(()),
            pltpu.SemaphoreType.DMA((2,)),
            pltpu.SemaphoreType.DMA((2,)),
            pltpu.SemaphoreType.DMA((2, widen)),
            pltpu.SemaphoreType.DMA((2, widen)),
            pltpu.SemaphoreType.DMA((2, widen, ranks - 1)),
            pltpu.SemaphoreType.DMA((2, widen, ranks - 1)),
        ],
        compiler_params=pltpu.CompilerParams(
            collective_id=0, has_side_effects=True, vmem_limit_bytes=VMEM_BYTES
        ),
        name="spectra_exchange",
    )(voltages, taps, table)


def shards(voltages, taps):
    local_inputs = voltages.shape[0]
    lags, length = taps.shape
    frames = voltages.shape[1] // length
    widen = lax.axis_size("wide")
    ranks = lax.axis_size("tm")
    channels = length // 2 // widen
    norm = 1.0 / (frames * ranks)

    full = exchanged_spectra(voltages, taps, widen, ranks)
    return gram_rows(full, local_inputs, channels, norm)


def gram_rows(full, inputs, channels, norm):
    ranks, widen, parts, _, width = full.shape
    total = widen * inputs
    own = total // ranks
    step = SUBLANES
    pairs = step // 2
    span = width // 4
    first = (lax.axis_index("tm") * (own // inputs)).astype(jnp.int32).reshape(1)

    tiles = total // LANES
    sides = own // inputs
    pieces = [(t, h) for t in range(ranks) for h in range(parts)]

    def kernel(first_ref, ref, out_ref, grams):
        own_from = first_ref[0]

        source = lax.broadcasted_iota(jnp.int32, (width, 2 * width), 0)
        target = lax.broadcasted_iota(jnp.int32, (width, 2 * width), 1)
        lane = target % width
        partner = jnp.where((lane // span) % 2 == 0, lane + span, lane - span)
        swap = jnp.where((lane // span) % 2 == 0, 1.0, -1.0)
        swap = jnp.where(
            (source == partner) & (lane // (2 * span) == target // width), swap, 0.0
        ).astype(jnp.bfloat16)
        lane = lax.broadcasted_iota(jnp.int32, (own, width), 1)
        masks = [
            jnp.where(lane // (2 * span) == parity, 1.0, 0.0).astype(jnp.bfloat16)
            for parity in range(2)
        ]

        for j in range(pairs):
            at = pl.ds(j * inputs, inputs)
            whole = jnp.concatenate(
                [ref[t, :, h, at, :].reshape(total, width) for t, h in pieces], axis=1
            )
            mine = [
                ref[t, pl.ds(own_from, sides), h, at, :].reshape(own, width) for t, h in pieces
            ]
            swapped = lax.dot_general(
                jnp.concatenate(mine, axis=0), swap, (((1,), (0,)), ((), ())),
                preferred_element_type=jnp.float32,
            ).astype(jnp.bfloat16)
            left = []
            for parity in range(2):
                left.append(jnp.concatenate([x * masks[parity] for x in mine], axis=1))
                columns = swapped[:, parity * width : (parity + 1) * width]
                left.append(
                    jnp.concatenate(
                        [columns[i * own : (i + 1) * own] for i in range(len(pieces))], axis=1
                    )
                )
            gram = norm * lax.dot_general(
                jnp.concatenate(left, axis=0), whole, (((1,), (1,)), ((), ())),
                preferred_element_type=jnp.float32,
            )
            for parity in range(2):
                for r in range(2):
                    top = (2 * parity + r) * own
                    grams[2 * j + parity, r] = gram[top : top + own]

        for r in range(2):
            for l in range(tiles):
                at = pl.ds(l * LANES, LANES)
                lines = exchanged_sublanes(
                    [grams[k, r, :, at].reshape(own // SUBLANES, SUBLANES, LANES) for k in range(step)]
                )
                for i in range(SUBLANES):
                    out_ref[:, i, r, :, at] = lines[i]

    rows = pl.pallas_call(
        kernel,
        grid=(channels // step,),
        out_shape=jax.ShapeDtypeStruct((own // SUBLANES, SUBLANES, 2, channels, total), jnp.float32),
        in_specs=[
            pl.BlockSpec(memory_space=pltpu.SMEM),
            pl.BlockSpec((ranks, widen, parts, pairs * inputs, width), lambda i: (0, 0, 0, i, 0)),
        ],
        out_specs=pl.BlockSpec(
            (own // SUBLANES, SUBLANES, 2, step, total), lambda i: (0, 0, 0, i, 0)
        ),
        scratch_shapes=[pltpu.VMEM((step, 2, own, total), jnp.float32)],
        compiler_params=pltpu.CompilerParams(vmem_limit_bytes=VMEM_BYTES),
        name="gram",
    )(first, full)
    return rows.reshape(own, 2, channels, total)


def solution(mesh):
    placed = (P("wide", "tm"), P())
    return jax.shard_map(
        shards, mesh=mesh, in_specs=placed, out_specs=P("tm", None, "wide", None), check_vma=False
    )
```
